32 devices in a mesh: groups: 2 (over y), depth: 4 (over z), lat: 2 (over x), sub: 2 (over core).
Axes of the slice: x: 2, y: 2, z: 4, core: 2. Of those that a mesh axis runs over, the one named last changes fastest.
Arguments:
- scalar_field: float32 [8, 18, 512, 512], P(('groups', 'depth'), None, 'lat', 'sub'), parts along dimension 0, may hold values from -6 to 6
- bin_index: int32 [8, 16, 512, 512], P(('groups', 'depth'), None, 'lat', 'sub'), parts along dimension 0, may hold values from 0 to 31
- sample_counts: int32 [8, 2, 2], P(('groups', 'depth'), 'lat', 'sub'), parts along dimension 0, may hold values from 1 to 16, as said below
- view_order: int32 [8], P('groups'), parts along dimension 0, may hold values from 0 to 3, each once
- light_dir: float32 [3], replicated, may hold values from -3 to 3
- tf_color: float32 [3, 32], replicated, may hold values from 0.1 to 1
- tf_opacity: float32 [32], replicated, may hold values from 0.005 to 0.08
Outputs:
- final_image: float32 [4, 1024, 512], P(None, ('groups', 'lat'), 'sub'), parts along dimension 1
The draws below stay inside these ranges and needn't reach their ends.
There are 2 independent parts, one for each index of `groups`. The reference program is written for one: setup_inputs(seed, part) draws one part's arguments, and reference() takes and returns one part's arrays. A program takes and returns all parts, laid end to end along the dimension named above; an argument that names none is the same for every part. Nothing has to cross between parts.
Inputs may be any that keep to these rules, and one draw needn't show every extreme that they name: `sample_counts`: one brick and tile of each part has exactly 16. `view_order`: each brick index appears once.
All inputs are finite; a program needn't handle non-finite values.
Results may differ from the reference program's by a relative error of at most 0.0003.
Values sent between devices are 32-bit elements; how exact they have to be, the bound alone decides.
A program may use at most 128 MiB of HBM per device.

```python
import math
import jax
import jax.numpy as jnp
from jax import lax

CX = 256
CY = 256
CZ = 16
NBINS = 32
BZ = 4
BX = 2
BY = 2
NX = 512
NY = 512


def draw_sample_counts(key, part):
    first_key, second_key, third_key = jax.random.split(key, 3)
    first_draw = jax.random.randint(first_key, (BZ, BX, BY), 1, CZ + 1)
    second_draw = jax.random.randint(second_key, (BZ, BX, BY), 1, CZ + 1)
    lowest = jnp.minimum(first_draw, second_draw)
    chosen = jax.random.randint(third_key, (), 0, BZ * BX * BY)
    flat_ids = jnp.arange(BZ * BX * BY).reshape(BZ, BX, BY)
    return jnp.where(flat_ids == chosen, CZ, lowest).astype(jnp.int32)


def plant(drawn, own_key, smallest, high):
    longest = drawn.shape.index(max(drawn.shape))
    spots = []
    for shift in (0, 1):
        where = [jax.random.randint(jax.random.fold_in(own_key, axis), (), 0, length) for axis, length in enumerate(drawn.shape)]
        where[longest] = (where[longest] + shift) % drawn.shape[longest]
        spots.append(tuple(where))
    return drawn.at[spots[0]].set(smallest).at[spots[1]].set(high)


def level_of(stream_key, shape, cuts, low, high):
    def one(position, parts):
        steps = jax.random.uniform(jax.random.fold_in(jax.random.fold_in(stream_key, 6), position), (parts,), jnp.float32, low / len(cuts), high / len(cuts))
        return jnp.repeat(jnp.exp(steps), shape[position] // parts).reshape((-1,) + (1,) * (len(shape) - position - 1))

    level = one(*cuts[0])
    for cut in cuts[1:]:
        level = level * one(*cut)
    return level


def noise(rng, dims, spread, most, shards=(), held_as=jnp.bfloat16):
    factor_of = level_of(rng, dims, shards, -0.22, 0.18) if shards else 1.0
    array = jax.random.normal(rng, dims, jnp.float32) * spread * factor_of
    return jnp.minimum(jnp.maximum(array, -most), most).astype(held_as)


def setup_inputs(seed: int = 0, part: int = 0) -> dict:
    key_list = jax.random.split(jax.random.key(seed), 8)
    part_keys = jax.random.split(jax.random.fold_in(key_list[7], part), 8)
    return {
        "scalar_field": noise(part_keys[0], (BZ, CZ + 2, NX, NY), 1.0, 6.0, ((0, 4), (2, 2), (3, 2)), jnp.float32),
        "bin_index": plant(jax.random.randint(part_keys[1], (BZ, CZ, NX, NY), 0, NBINS), jax.random.fold_in(part_keys[1], 1), 0, NBINS - 1).astype(jnp.int32),
        "sample_counts": draw_sample_counts(jax.random.fold_in(jax.random.fold_in(key_list[7], part), 71), part),
        "view_order": jax.random.permutation(part_keys[3], BZ).astype(jnp.int32),
        "light_dir": noise(key_list[4], (3,), 1.0, 3.0, (), jnp.float32),
        "tf_color": jnp.clip(jax.random.uniform(key_list[5], (3, NBINS), jnp.float32, 0.1, 1.0), 0.1, 1.0),
        "tf_opacity": jnp.clip(jnp.exp(jax.random.uniform(key_list[6], (NBINS,), jnp.float32, math.log(0.005), math.log(0.08))), 0.005, 0.08),
    }


def shading_terms(padded, depth_step, light_dir):
    below_plane = lax.dynamic_index_in_dim(padded, depth_step, 0, keepdims=False)[1:-1, 1:-1]
    centre_pad = lax.dynamic_index_in_dim(padded, depth_step + 1, 0, keepdims=False)
    above_plane = lax.dynamic_index_in_dim(padded, depth_step + 2, 0, keepdims=False)[1:-1, 1:-1]
    centre = centre_pad[1:-1, 1:-1]
    grad_x = (centre_pad[2:, 1:-1] - centre_pad[:-2, 1:-1]) * 0.5
    grad_y = (centre_pad[1:-1, 2:] - centre_pad[1:-1, :-2]) * 0.5
    grad_z = (above_plane - below_plane) * 0.5
    facing = (grad_x * light_dir[0] + grad_y * light_dir[1] + grad_z * light_dir[2]) / jnp.sqrt(grad_x * grad_x + grad_y * grad_y + grad_z * grad_z + 1.0)
    shading = 0.25 + 0.5 * jnp.abs(facing)
    return (centre, shading)

def composite(stacked, view_order):
    accum_rgb = jnp.zeros(stacked.shape[1:2 - 1] + (3,) + stacked.shape[2:], jnp.float32)
    remain = jnp.ones(stacked.shape[2:], jnp.float32)

    def one_brick(rank_idx, state):
        image_rgb, image_remain = state
        partial_value = lax.dynamic_index_in_dim(stacked, view_order[rank_idx], 0, keepdims=False)
        return (image_rgb + image_remain * partial_value[:3], image_remain * partial_value[3])
    image_rgb, image_remain = lax.fori_loop(0, stacked.shape[0], one_brick, (accum_rgb, remain))
    return jnp.concatenate([image_rgb, (1.0 - image_remain)[None]], 0)

def reference(scalar_field, bin_index, sample_counts, view_order, light_dir, tf_color, tf_opacity):

    def march_brick(brick_idx):
        field_brick = lax.dynamic_index_in_dim(scalar_field, brick_idx, 0, keepdims=False)
        padded = jnp.pad(field_brick, ((0, 0), (1, 1), (1, 1)))
        bins_brick = lax.dynamic_index_in_dim(bin_index, brick_idx, 0, keepdims=False)
        tile_counts = lax.dynamic_index_in_dim(sample_counts, brick_idx, 0, keepdims=False)
        count_map = jnp.repeat(jnp.repeat(tile_counts, CX, axis=0), CY, axis=1).astype(jnp.int32)

        def one_plane(depth_step, state):
            accum_rgb, remain = state
            centre, shading = shading_terms(padded, depth_step, light_dir)
            bins_plane = lax.dynamic_index_in_dim(bins_brick, depth_step, 0, keepdims=False)
            colour = jnp.take(tf_color, bins_plane, axis=1)
            extinct = jnp.take(tf_opacity, bins_plane)
            inside = (depth_step < count_map).astype(jnp.float32)
            density = extinct * jax.nn.softplus(centre) * inside
            survive = jnp.exp(-density)
            opacity_now = 1.0 - survive
            accum_rgb = accum_rgb + remain * (colour * (shading * opacity_now)[None])
            return (accum_rgb, remain * survive)
        init = (jnp.zeros((3,) + count_map.shape, jnp.float32), jnp.ones(count_map.shape, jnp.float32))
        accum_rgb, remain = lax.fori_loop(0, CZ, one_plane, init)
        return jnp.concatenate([accum_rgb, remain[None]], 0)
    stacked = lax.map(march_brick, jnp.arange(BZ, dtype=jnp.int32))
    return composite(stacked, view_order)
```

```python
import functools
import math

import jax
import jax.numpy as jnp
from jax import lax
from jax.experimental import pallas as pl
from jax.experimental.pallas import tpu as pltpu
from jax.sharding import PartitionSpec as P

MESH = pl.DeviceIdType.MESH
LANES = 128
STRIPS = 8
LAG_SUM = 1
LAG_DONE = 2


def composite(stacked, view_order):
    image_rgb = jnp.zeros((3,) + stacked.shape[2:], jnp.float32)
    image_remain = jnp.ones(stacked.shape[2:], jnp.float32)

    def one_brick(rank_idx, state):
        accum_rgb, remain = state
        partial_value = lax.dynamic_index_in_dim(stacked, view_order[rank_idx], 0, keepdims=False)
        return (accum_rgb + remain * partial_value[:3], remain * partial_value[3])

    image_rgb, image_remain = lax.fori_loop(
        0, stacked.shape[0], one_brick, (image_rgb, image_remain)
    )
    return jnp.concatenate([image_rgb, (1.0 - image_remain)[None]], 0)


def lookup(table, bins):
    return jnp.take_along_axis(table, bins, axis=1, mode="promise_in_bounds")


def kernel(
    n_depth, n_lat, exchange,
    field, bins, counts, order, light, color, opacity, out,
    fv, bv, col_send, col_recv, row_send, row_recv, table,
    part, ends, far_remain, mine, theirs, fin,
    load_sem, col_sem, row_sem, barrier_pad,
    part_sems, part_recv, own_sems, own_recv, far_sems, far_recv,
    sum_sems, sum_recv, fin_sems, fin_recv, out_sems,
):
    planes = bv.shape[1]
    rows = bv.shape[2]
    strip = rows // STRIPS
    z = lax.axis_index("depth")
    lat = lax.axis_index("lat")
    sub = lax.axis_index("sub")

    loads = []
    for t in range(2):
        loads.append(pltpu.make_async_copy(
            field.at[0, :, :, pl.ds(t * LANES, LANES)],
            fv.at[t, :, pl.ds(8, rows), :], load_sem.at[t]))
    for t in range(2):
        loads.append(pltpu.make_async_copy(
            bins.at[0, :, :, pl.ds(t * LANES, LANES)], bv.at[t], load_sem.at[2 + t]))
    for load in loads:
        load.start()

    barrier = pltpu.get_barrier_semaphore()
    pl.semaphore_signal(barrier, inc=1, device_id={"sub": 1 - sub}, device_id_type=MESH)
    has_up = lat > 0
    has_down = lat < n_lat - 1

    @pl.when(has_up)
    def _():
        pl.semaphore_signal(barrier, inc=1, device_id={"lat": lat - 1}, device_id_type=MESH)

    @pl.when(has_down)
    def _():
        pl.semaphore_signal(barrier, inc=1, device_id={"lat": lat + 1}, device_id_type=MESH)

    greet = 1 + has_up.astype(jnp.int32) + has_down.astype(jnp.int32)
    is_end = jnp.logical_or(z == 0, z == 3)
    is_mid = jnp.logical_not(is_end)
    left = z < 2
    near = jnp.where(z == 0, 1, jnp.where(z == 1, 0, jnp.where(z == 2, 3, 2)))
    peer = 3 - z
    across = jnp.where(z == 0, 2, jnp.where(z == 1, 3, jnp.where(z == 2, 0, 1)))
    if exchange:
        pl.semaphore_signal(barrier, inc=1, device_id={"depth": near}, device_id_type=MESH)
        pl.semaphore_signal(barrier, inc=1, device_id={"depth": across}, device_id_type=MESH)

        @pl.when(is_mid)
        def _():
            pl.semaphore_signal(barrier, inc=1, device_id={"depth": peer}, device_id_type=MESH)

        greet = greet + 2 + is_mid.astype(jnp.int32)

    lane = lax.broadcasted_iota(jnp.int32, (8, LANES), 1)
    first_lane = lane == 0
    last_lane = lane == LANES - 1

    table[...] = jnp.zeros_like(table)
    n_bins = color.shape[1]
    for c in range(3):
        table[c, :, 0:n_bins] = jnp.broadcast_to(color[c:c + 1, :], (8, n_bins))
    table[3, :, 0:n_bins] = jnp.broadcast_to(
        opacity[...].reshape(1, n_bins), (8, n_bins)) * (-1.0 / math.log(2.0))

    loads[0].wait()
    loads[1].wait()

    for t in range(2):
        for k in range(planes):
            row_send[0, t, k:k + 1, :] = fv[t, k + 1, 8:9, :]
            row_send[1, t, k:k + 1, :] = fv[t, k + 1, 7 + rows:8 + rows, :]

    pl.semaphore_wait(barrier, greet)

    up = pltpu.make_async_remote_copy(
        src_ref=row_send.at[0], dst_ref=row_recv.at[1], send_sem=row_sem.at[0],
        recv_sem=row_sem.at[2], device_id={"lat": lat - 1}, device_id_type=MESH)
    down = pltpu.make_async_remote_copy(
        src_ref=row_send.at[1], dst_ref=row_recv.at[0], send_sem=row_sem.at[1],
        recv_sem=row_sem.at[3], device_id={"lat": lat + 1}, device_id_type=MESH)

    @pl.when(has_up)
    def _():
        up.start()

    @pl.when(has_down)
    def _():
        down.start()

    def pack(src, offset):
        def chunk(i, _):
            r0 = pl.multiple_of(i * 8, 8)
            packed = jnp.zeros((8, LANES), jnp.float32)
            for k in range(planes):
                to = (2 * k + offset) % LANES
                shift = (to + 1) % LANES if src == 1 else to
                value = fv[src, k + 1, pl.ds(8 + r0, 8), :]
                if shift:
                    value = pltpu.roll(value, shift, 1)
                packed = jnp.where(lane == to, value, packed)
            col_send[pl.ds(r0, 8), :] = packed
            return 0
        lax.fori_loop(0, rows // 8, chunk, 0)

    @pl.when(sub == 0)
    def _():
        pack(1, 0)

    @pl.when(sub == 1)
    def _():
        pack(0, -1)

    side = pltpu.make_async_remote_copy(
        src_ref=col_send, dst_ref=col_recv, send_sem=col_sem.at[0],
        recv_sem=col_sem.at[1], device_id={"sub": 1 - sub}, device_id_type=MESH)
    side.start()

    @pl.when(has_up)
    def _():
        up.wait_send()
        down.wait_recv()

    @pl.when(has_down)
    def _():
        down.wait_send()
        up.wait_recv()

    @pl.when(jnp.logical_not(has_up))
    def _():
        row_recv[0] = jnp.zeros(row_recv.shape[1:], jnp.float32)

    @pl.when(jnp.logical_not(has_down))
    def _():
        row_recv[1] = jnp.zeros(row_recv.shape[1:], jnp.float32)

    for t in range(2):
        for k in range(planes):
            fv[t, k + 1, 7:8, :] = row_recv[0, t, k:k + 1, :]
            fv[t, k + 1, 8 + rows:9 + rows, :] = row_recv[1, t, k:k + 1, :]

    loads[2].wait()
    loads[3].wait()
    side.wait()

    lx = light[0] * 0.5
    ly = light[1] * 0.5
    lz = light[2] * 0.5
    count = counts[0, 0, 0]

    def march(r0):
        halo = col_recv[pl.ds(r0, 8), :]
        before = [fv[t, 0, pl.ds(8 + r0, 8), :] for t in range(2)]
        here = [fv[t, 1, pl.ds(8 + r0, 8), :] for t in range(2)]
        total = [[jnp.zeros((8, LANES), jnp.float32) for _ in range(3)] for _ in range(2)]
        remain = [jnp.ones((8, LANES), jnp.float32) for _ in range(2)]
        colors = [table[c] for c in range(3)]
        extinct = table[3]
        for k in range(planes):
            after = [fv[t, k + 2, pl.ds(8 + r0, 8), :] for t in range(2)]
            extinct_k = jnp.where(k < count, extinct, 0.0)
            up1 = [pltpu.roll(here[t], 1, 1) for t in range(2)]
            dn1 = [pltpu.roll(here[t], LANES - 1, 1) for t in range(2)]
            minus = [jnp.where(first_lane, halo, up1[0]), jnp.where(first_lane, up1[0], up1[1])]
            plus = [jnp.where(last_lane, dn1[1], dn1[0]), jnp.where(last_lane, halo, dn1[1])]
            for t in range(2):
                gx = fv[t, k + 1, pl.ds(9 + r0, 8), :] - fv[t, k + 1, pl.ds(7 + r0, 8), :]
                gy = plus[t] - minus[t]
                gz = after[t] - before[t]
                dot = gx * lx + gy * ly + gz * lz
                norm = gx * gx + gy * gy + (gz * gz + 4.0)
                shading = jnp.abs(dot * lax.rsqrt(norm)) + 0.25
                soft = jnp.log(1.0 + jnp.exp(here[t]))
                bin_ids = bv[t, k, pl.ds(r0, 8), :]
                survive = jnp.exp2(lookup(extinct_k, bin_ids) * soft)
                left_over = remain[t] * survive
                weight = (remain[t] - left_over) * shading
                for c in range(3):
                    total[t][c] = total[t][c] + weight * lookup(colors[c], bin_ids)
                remain[t] = left_over
            before, here = here, after
            halo = pltpu.roll(halo, LANES - 2, 1)
        for t in range(2):
            for c in range(3):
                part[c, pl.ds(r0, 8), t * LANES:(t + 1) * LANES] = total[t][c]
            part[3, pl.ds(r0, 8), t * LANES:(t + 1) * LANES] = remain[t]

    def compute(s):
        def group(i, _):
            march(pl.multiple_of(s * strip + i * 8, 8))
            return 0
        lax.fori_loop(0, strip // 8, group, 0)

    def at_rows(s):
        return pl.ds(pl.multiple_of(s * strip, strip), strip)

    def to_out(s, src):
        return pltpu.make_async_copy(
            src.at[:, at_rows(s), :], out.at[:, at_rows(s), :], out_sems.at[s])

    if not exchange:
        def plain(s, _):
            compute(s)
            to_out(s, part).start()
            return 0
        lax.fori_loop(0, STRIPS, plain, 0)

        def finish(s, _):
            to_out(s, part).wait()
            return 0
        lax.fori_loop(0, STRIPS, finish, 0)
        return

    def send_part(s):
        return pltpu.make_async_remote_copy(
            src_ref=part.at[:, at_rows(s), :], dst_ref=ends.at[:, at_rows(s), :],
            send_sem=part_sems.at[s], recv_sem=part_recv.at[s],
            device_id={"depth": near}, device_id_type=MESH)

    def send_far(s):
        return pltpu.make_async_remote_copy(
            src_ref=part.at[3, at_rows(s), :], dst_ref=far_remain.at[1, at_rows(s), :],
            send_sem=far_sems.at[s], recv_sem=far_recv.at[s],
            device_id={"depth": across}, device_id_type=MESH)

    def send_own(s):
        return pltpu.make_async_remote_copy(
            src_ref=part.at[3, at_rows(s), :], dst_ref=far_remain.at[0, at_rows(s), :],
            send_sem=own_sems.at[s], recv_sem=own_recv.at[s],
            device_id={"depth": peer}, device_id_type=MESH)

    def send_sum(s):
        return pltpu.make_async_remote_copy(
            src_ref=mine.at[:, at_rows(s), :], dst_ref=theirs.at[:, at_rows(s), :],
            send_sem=sum_sems.at[s], recv_sem=sum_recv.at[s],
            device_id={"depth": peer}, device_id_type=MESH)

    def send_fin(s):
        return pltpu.make_async_remote_copy(
            src_ref=fin.at[:, at_rows(s), :], dst_ref=out.at[:, at_rows(s), :],
            send_sem=fin_sems.at[s], recv_sem=fin_recv.at[s],
            device_id={"depth": near}, device_id_type=MESH)

    @pl.when(is_end)
    def _():
        def first(s, _):
            compute(s)
            send_far(s).start()
            send_part(s).start()
            return 0
        lax.fori_loop(0, STRIPS, first, 0)

        def last(s, _):
            send_far(s).wait_send()
            send_part(s).wait_send()
            send_fin(s).wait_recv()
            return 0
        lax.fori_loop(0, STRIPS, last, 0)

    def rank_of(brick):
        rank = jnp.int32(0)
        for r in range(1, n_depth):
            rank = rank + jnp.where(order[r] == brick, r, 0)
        return rank

    rank_mine = rank_of(z)
    rank_near = rank_of(near)
    rank_peer = rank_of(peer)
    rank_across = rank_of(across)

    def sums(s):
        def group(i, _):
            r = pl.ds(pl.multiple_of(s * strip + i * 8, 8), 8)
            one = jnp.ones((8, part.shape[2]), jnp.float32)
            own = part[3, r, :]
            end = ends[3, r, :]
            there = far_remain[0, r, :]
            far = far_remain[1, r, :]

            def gate(a, b, value):
                return jnp.where(a < b, value, one)

            w_own = (gate(rank_near, rank_mine, end) * gate(rank_peer, rank_mine, there)
                     * gate(rank_across, rank_mine, far))
            w_end = (gate(rank_mine, rank_near, own) * gate(rank_peer, rank_near, there)
                     * gate(rank_across, rank_near, far))
            for c in range(3):
                mine[c, r, :] = w_own * part[c, r, :] + w_end * ends[c, r, :]
            fin[3, r, :] = 1.0 - (own * end) * (there * far)
            return 0
        lax.fori_loop(0, strip // 8, group, 0)

    def done(s):
        def group(i, _):
            r = pl.ds(pl.multiple_of(s * strip + i * 8, 8), 8)
            for c in range(3):
                fin[c, r, :] = mine[c, r, :] + theirs[c, r, :]
            return 0
        lax.fori_loop(0, strip // 8, group, 0)

    @pl.when(is_mid)
    def _():
        def stage(it, _):
            @pl.when(it < STRIPS)
            def _():
                compute(it)
                send_own(it).start()

            @pl.when(jnp.logical_and(it >= LAG_SUM, it < STRIPS + LAG_SUM))
            def _():
                s = it - LAG_SUM
                send_part(s).wait_recv()
                send_far(s).wait_recv()
                send_own(s).wait_recv()
                sums(s)
                send_sum(s).start()

            @pl.when(it >= LAG_DONE)
            def _():
                s = it - LAG_DONE
                send_sum(s).wait_recv()
                done(s)
                send_fin(s).start()
                to_out(s, fin).start()
            return 0
        lax.fori_loop(0, STRIPS + LAG_DONE, stage, 0)

        def last(s, _):
            send_own(s).wait_send()
            send_sum(s).wait_send()
            send_fin(s).wait_send()
            to_out(s, fin).wait()
            return 0
        lax.fori_loop(0, STRIPS, last, 0)


def on_device(n_depth, n_lat, scalar_field, bin_index, sample_counts, view_order, light_dir,
              tf_color, tf_opacity):
    exchange = n_depth == 4
    planes, rows, cols = bin_index.shape[1:]
    image = (4, rows, cols)
    dma = pltpu.SemaphoreType.DMA
    smem = pl.BlockSpec(memory_space=pltpu.SMEM)
    vmem = pl.BlockSpec(memory_space=pltpu.VMEM)
    hbm = pl.BlockSpec(memory_space=pl.ANY)
    f32 = jnp.float32
    result = pl.pallas_call(
        functools.partial(kernel, n_depth, n_lat, exchange),
        out_shape=jax.ShapeDtypeStruct(image, f32),
        in_specs=[hbm, hbm, smem, smem, smem, vmem, vmem],
        out_specs=hbm,
        scratch_shapes=[
            pltpu.VMEM((2, planes + 2, rows + 16, LANES), f32),
            pltpu.VMEM((2, planes, rows, LANES), jnp.int32),
            pltpu.VMEM((rows, LANES), f32),
            pltpu.VMEM((rows, LANES), f32),
            pltpu.VMEM((2, 2, planes, LANES), f32),
            pltpu.VMEM((2, 2, planes, LANES), f32),
            pltpu.VMEM((4, 8, LANES), f32),
            pltpu.VMEM(image, f32),
            pltpu.VMEM(image, f32),
            pltpu.VMEM((2, rows, cols), f32),
            pltpu.VMEM((3, rows, cols), f32),
            pltpu.VMEM((3, rows, cols), f32),
            pltpu.VMEM(image, f32),
            dma((4,)), dma((2,)), dma((4,)), dma((1,)),
        ] + [dma((STRIPS,))] * 11,
        compiler_params=pltpu.CompilerParams(
            collective_id=0, has_side_effects=True, vmem_limit_bytes=48 * 1024 * 1024),
    )(scalar_field, bin_index, sample_counts, view_order, light_dir, tf_color, tf_opacity)
    if exchange:
        return result
    return composite(lax.all_gather(result[None], "depth", axis=0, tiled=True), view_order)


def solution(mesh):
    return jax.shard_map(
        functools.partial(on_device, mesh.shape["depth"], mesh.shape["lat"]),
        mesh=mesh,
        in_specs=(
            P(("groups", "depth"), None, "lat", "sub"),
            P(("groups", "depth"), None, "lat", "sub"),
            P(("groups", "depth"), "lat", "sub"),
            P("groups"),
            P(),
            P(),
            P(),
        ),
        out_specs=P(None, ("groups", "lat"), "sub"),
        check_vma=False,
    )
```

```python
import functools
import math

import jax
import jax.numpy as jnp
from jax import lax
from jax.experimental import pallas as pl
from jax.experimental.pallas import tpu as pltpu
from jax.sharding import PartitionSpec as P

MESH = pl.DeviceIdType.MESH
LANES = 128
STRIPS = 16
CHUNKS = 4
LAG_DONE = 3


def composite(stacked, view_order):
    image_rgb = jnp.zeros((3,) + stacked.shape[2:], jnp.float32)
    image_remain = jnp.ones(stacked.shape[2:], jnp.float32)

    def one_brick(rank_idx, state):
        accum_rgb, remain = state
        partial_value = lax.dynamic_index_in_dim(stacked, view_order[rank_idx], 0, keepdims=False)
        return (accum_rgb + remain * partial_value[:3], remain * partial_value[3])

    image_rgb, image_remain = lax.fori_loop(
        0, stacked.shape[0], one_brick, (image_rgb, image_remain)
    )
    return jnp.concatenate([image_rgb, (1.0 - image_remain)[None]], 0)


def lookup(table, bins):
    return jnp.take_along_axis(table, bins, axis=1, mode="promise_in_bounds")


def kernel(
    n_depth, n_lat, exchange,
    field, bins, counts_in, order_in, light_in, color_in, opacity_in, out,
    counts, order, light, color, opacity, small_sem, fv, bv, col_send, col_recv, row_send, row_recv, table,
    part, ends, far_remain, mine, theirs, fin,
    load_sem, col_sem, row_sem,
    part_sems, part_recv, own_sems, own_recv, end_sems, end_recv, far_sems, far_recv,
    sum_sems, sum_recv, opac_sems, opac_recv, fin_sems, fin_recv, out_sems, out_opac_sems,
):
    planes = bv.shape[1]
    rows = bv.shape[2]
    strip = rows // STRIPS
    z = lax.axis_index("depth")
    lat = lax.axis_index("lat")
    sub = lax.axis_index("sub")

    small = [
        pltpu.make_async_copy(src, dst, small_sem.at[i])
        for i, (src, dst) in enumerate((
            (counts_in, counts), (order_in, order), (light_in, light),
            (color_in, color), (opacity_in, opacity)))
    ]
    for load in small:
        load.start()

    chunk_rows = rows // CHUNKS
    loads = []
    for c in range(CHUNKS):
        for t in range(2):
            loads.append(pltpu.make_async_copy(
                field.at[0, :, pl.ds(c * chunk_rows, chunk_rows), pl.ds(t * LANES, LANES)],
                fv.at[t, :, pl.ds(8 + c * chunk_rows, chunk_rows), :], load_sem.at[c, t]))
            loads.append(pltpu.make_async_copy(
                bins.at[0, :, pl.ds(c * chunk_rows, chunk_rows), pl.ds(t * LANES, LANES)],
                bv.at[t, :, pl.ds(c * chunk_rows, chunk_rows), :], load_sem.at[c, 2 + t]))
    for load in loads:
        load.start()

    barrier = pltpu.get_barrier_semaphore()
    pl.semaphore_signal(barrier, inc=1, device_id={"sub": 1 - sub}, device_id_type=MESH)
    has_up = lat > 0
    has_down = lat < n_lat - 1

    @pl.when(has_up)
    def _():
        pl.semaphore_signal(barrier, inc=1, device_id={"lat": lat - 1}, device_id_type=MESH)

    @pl.when(has_down)
    def _():
        pl.semaphore_signal(barrier, inc=1, device_id={"lat": lat + 1}, device_id_type=MESH)

    greet = 1 + has_up.astype(jnp.int32) + has_down.astype(jnp.int32)
    is_end = jnp.logical_or(z == 0, z == 3)
    is_mid = jnp.logical_not(is_end)
    near = jnp.where(z == 0, 1, jnp.where(z == 1, 0, jnp.where(z == 2, 3, 2)))
    peer = 3 - z
    across = 3 - near
    if exchange:
        pl.semaphore_signal(barrier, inc=1, device_id={"depth": near}, device_id_type=MESH)

        @pl.when(is_mid)
        def _():
            pl.semaphore_signal(barrier, inc=1, device_id={"depth": peer}, device_id_type=MESH)

        greet = greet + 1 + is_mid.astype(jnp.int32)

    lane = lax.broadcasted_iota(jnp.int32, (8, LANES), 1)
    first_lane = lane == 0
    last_lane = lane == LANES - 1

    for load in small:
        load.wait()
    table[...] = jnp.zeros_like(table)
    n_bins = color.shape[1]
    for c in range(3):
        table[c, :, 0:n_bins] = jnp.broadcast_to(color[c:c + 1, :], (8, n_bins))
    table[3, :, 0:n_bins] = jnp.broadcast_to(
        opacity[...].reshape(1, n_bins), (8, n_bins)) * (-1.0 / math.log(2.0))

    count = counts[0, 0, 0]

    def at_rows(s):
        return pl.ds(pl.multiple_of(s * strip, strip), strip)

    def send_own(s):
        return pltpu.make_async_remote_copy(
            src_ref=part.at[3, at_rows(s), :], dst_ref=far_remain.at[0, at_rows(s), :],
            send_sem=own_sems.at[s], recv_sem=own_recv.at[s],
            device_id={"depth": peer}, device_id_type=MESH)

    def send_end(s):
        return pltpu.make_async_remote_copy(
            src_ref=part.at[3, at_rows(s), :], dst_ref=ends.at[3, at_rows(s), :],
            send_sem=end_sems.at[s], recv_sem=end_recv.at[s],
            device_id={"depth": near}, device_id_type=MESH)

    def send_far(s):
        return pltpu.make_async_remote_copy(
            src_ref=ends.at[3, at_rows(s), :], dst_ref=far_remain.at[1, at_rows(s), :],
            send_sem=far_sems.at[s], recv_sem=far_recv.at[s],
            device_id={"depth": peer}, device_id_type=MESH)

    def survive_all(s, _):
        def group(i, _):
            r0 = pl.multiple_of(s * strip + i * 8, 8)
            for t in range(2):
                power = jnp.zeros((8, LANES), jnp.float32)
                for k in range(planes):
                    extinct_k = jnp.where(k < count, table[3], 0.0)
                    soft = jnp.log(1.0 + jnp.exp(fv[t, k + 1, pl.ds(8 + r0, 8), :]))
                    power = power + lookup(extinct_k, bv[t, k, pl.ds(r0, 8), :]) * soft
                part[3, pl.ds(r0, 8), t * LANES:(t + 1) * LANES] = jnp.exp2(power)
            return 0
        lax.fori_loop(0, strip // 8, group, 0)
        if exchange:
            @pl.when(is_end)
            def _():
                send_end(s).start()

            @pl.when(is_mid)
            def _():
                send_own(s).start()
        return 0

    def remains(c):
        for load in loads[4 * c:4 * c + 4]:
            load.wait()
        lax.fori_loop(c * STRIPS // CHUNKS, (c + 1) * STRIPS // CHUNKS, survive_all, 0)

    pl.semaphore_wait(barrier, greet)
    for c in range(CHUNKS // 2):
        remains(c)
    for load in loads[2 * CHUNKS:]:
        load.wait()

    for t in range(2):
        for k in range(planes):
            row_send[0, t, k:k + 1, :] = fv[t, k + 1, 8:9, :]
            row_send[1, t, k:k + 1, :] = fv[t, k + 1, 7 + rows:8 + rows, :]

    up = pltpu.make_async_remote_copy(
        src_ref=row_send.at[0], dst_ref=row_recv.at[1], send_sem=row_sem.at[0],
        recv_sem=row_sem.at[2], device_id={"lat": lat - 1}, device_id_type=MESH)
    down = pltpu.make_async_remote_copy(
        src_ref=row_send.at[1], dst_ref=row_recv.at[0], send_sem=row_sem.at[1],
        recv_sem=row_sem.at[3], device_id={"lat": lat + 1}, device_id_type=MESH)

    @pl.when(has_up)
    def _():
        up.start()

    @pl.when(has_down)
    def _():
        down.start()

    def pack(src, offset):
        def chunk(i, _):
            r0 = pl.multiple_of(i * 8, 8)
            packed = jnp.zeros((8, LANES), jnp.float32)
            for k in range(planes):
                to = (2 * k + offset) % LANES
                shift = (to + 1) % LANES if src == 1 else to
                value = fv[src, k + 1, pl.ds(8 + r0, 8), :]
                if shift:
                    value = pltpu.roll(value, shift, 1)
                packed = jnp.where(lane == to, value, packed)
            col_send[pl.ds(r0, 8), :] = packed
            return 0
        lax.fori_loop(0, rows // 8, chunk, 0)

    @pl.when(sub == 0)
    def _():
        pack(1, 0)

    @pl.when(sub == 1)
    def _():
        pack(0, -1)

    side = pltpu.make_async_remote_copy(
        src_ref=col_send, dst_ref=col_recv, send_sem=col_sem.at[0],
        recv_sem=col_sem.at[1], device_id={"sub": 1 - sub}, device_id_type=MESH)
    side.start()

    for c in range(CHUNKS // 2, CHUNKS):
        lax.fori_loop(c * STRIPS // CHUNKS, (c + 1) * STRIPS // CHUNKS, survive_all, 0)

    @pl.when(has_up)
    def _():
        up.wait_send()
        down.wait_recv()

    @pl.when(has_down)
    def _():
        down.wait_send()
        up.wait_recv()

    @pl.when(jnp.logical_not(has_up))
    def _():
        row_recv[0] = jnp.zeros(row_recv.shape[1:], jnp.float32)

    @pl.when(jnp.logical_not(has_down))
    def _():
        row_recv[1] = jnp.zeros(row_recv.shape[1:], jnp.float32)

    for t in range(2):
        for k in range(planes):
            fv[t, k + 1, 7:8, :] = row_recv[0, t, k:k + 1, :]
            fv[t, k + 1, 8 + rows:9 + rows, :] = row_recv[1, t, k:k + 1, :]

    if exchange:
        @pl.when(is_mid)
        def _():
            def forward(s, _):
                send_end(s).wait_recv()
                send_far(s).start()
                return 0
            lax.fori_loop(0, STRIPS, forward, 0)

    side.wait()

    lx = light[0] * 0.5
    ly = light[1] * 0.5
    lz = light[2] * 0.5

    def march(r0):
        halo = col_recv[pl.ds(r0, 8), :]
        before = [fv[t, 0, pl.ds(8 + r0, 8), :] for t in range(2)]
        here = [fv[t, 1, pl.ds(8 + r0, 8), :] for t in range(2)]
        total = [[jnp.zeros((8, LANES), jnp.float32) for _ in range(3)] for _ in range(2)]
        remain = [jnp.ones((8, LANES), jnp.float32) for _ in range(2)]
        colors = [table[c] for c in range(3)]
        extinct = table[3]
        for k in range(planes):
            after = [fv[t, k + 2, pl.ds(8 + r0, 8), :] for t in range(2)]
            extinct_k = jnp.where(k < count, extinct, 0.0)
            up1 = [pltpu.roll(here[t], 1, 1) for t in range(2)]
            dn1 = [pltpu.roll(here[t], LANES - 1, 1) for t in range(2)]
            edge = pltpu.roll(halo, (LANES - 2 * k) % LANES, 1) if k else halo
            minus = [jnp.where(first_lane, edge, up1[0]), jnp.where(first_lane, up1[0], up1[1])]
            plus = [jnp.where(last_lane, dn1[1], dn1[0]), jnp.where(last_lane, edge, dn1[1])]
            for t in range(2):
                gx = fv[t, k + 1, pl.ds(9 + r0, 8), :] - fv[t, k + 1, pl.ds(7 + r0, 8), :]
                gy = plus[t] - minus[t]
                gz = after[t] - before[t]
                dot = gx * lx + gy * ly + gz * lz
                norm = gx * gx + gy * gy + (gz * gz + 4.0)
                shading = jnp.abs(dot * lax.rsqrt(norm)) + 0.25
                soft = jnp.log(1.0 + jnp.exp(here[t]))
                bin_ids = bv[t, k, pl.ds(r0, 8), :]
                survive = jnp.exp2(lookup(extinct_k, bin_ids) * soft)
                left_over = remain[t] * survive
                weight = (remain[t] - left_over) * shading
                for c in range(3):
                    total[t][c] = total[t][c] + weight * lookup(colors[c], bin_ids)
                remain[t] = left_over
            before, here = here, after
        for t in range(2):
            for c in range(3):
                part[c, pl.ds(r0, 8), t * LANES:(t + 1) * LANES] = total[t][c]

    def compute(s):
        def group(i, _):
            march(pl.multiple_of(s * strip + i * 8, 8))
            return 0
        lax.fori_loop(0, strip // 8, group, 0)

    def to_out(s, src):
        return pltpu.make_async_copy(
            src.at[:, at_rows(s), :], out.at[:, at_rows(s), :], out_sems.at[s])

    if not exchange:
        def plain(s, _):
            compute(s)
            to_out(s, part).start()
            return 0
        lax.fori_loop(0, STRIPS, plain, 0)

        def finish(s, _):
            to_out(s, part).wait()
            return 0
        lax.fori_loop(0, STRIPS, finish, 0)
        return

    def send_part(s):
        return pltpu.make_async_remote_copy(
            src_ref=part.at[0:3, at_rows(s), :], dst_ref=ends.at[0:3, at_rows(s), :],
            send_sem=part_sems.at[s], recv_sem=part_recv.at[s],
            device_id={"depth": near}, device_id_type=MESH)

    def send_sum(s):
        return pltpu.make_async_remote_copy(
            src_ref=mine.at[:, at_rows(s), :], dst_ref=theirs.at[:, at_rows(s), :],
            send_sem=sum_sems.at[s], recv_sem=sum_recv.at[s],
            device_id={"depth": peer}, device_id_type=MESH)

    def send_fin(s):
        return pltpu.make_async_remote_copy(
            src_ref=fin.at[0:3, at_rows(s), :], dst_ref=out.at[0:3, at_rows(s), :],
            send_sem=fin_sems.at[s], recv_sem=fin_recv.at[s],
            device_id={"depth": near}, device_id_type=MESH)

    def send_opac(s):
        return pltpu.make_async_remote_copy(
            src_ref=fin.at[3, at_rows(s), :], dst_ref=out.at[3, at_rows(s), :],
            send_sem=opac_sems.at[s], recv_sem=opac_recv.at[s],
            device_id={"depth": near}, device_id_type=MESH)

    def rgb_out(s):
        return pltpu.make_async_copy(
            fin.at[0:3, at_rows(s), :], out.at[0:3, at_rows(s), :], out_sems.at[s])

    def opac_out(s):
        return pltpu.make_async_copy(
            fin.at[3, at_rows(s), :], out.at[3, at_rows(s), :], out_opac_sems.at[s])

    @pl.when(is_end)
    def _():
        def first(s, _):
            compute(s)
            send_part(s).start()
            return 0
        lax.fori_loop(0, STRIPS, first, 0)

        def last(s, _):
            send_end(s).wait_send()
            send_part(s).wait_send()
            send_opac(s).wait_recv()
            send_fin(s).wait_recv()
            return 0
        lax.fori_loop(0, STRIPS, last, 0)

    def rank_of(brick):
        rank = jnp.int32(0)
        for r in range(1, n_depth):
            rank = rank + jnp.where(order[r] == brick, r, 0)
        return rank

    rank_mine = rank_of(z)
    rank_near = rank_of(near)
    rank_peer = rank_of(peer)
    rank_across = rank_of(across)

    def gate(a, b, value):
        return jnp.where(a < b, value, jnp.ones_like(value))

    def sums(s):
        r = at_rows(s)
        own = part[3, r, :]
        end = ends[3, r, :]
        there = far_remain[0, r, :]
        far = far_remain[1, r, :]
        w_own = (gate(rank_near, rank_mine, end) * gate(rank_peer, rank_mine, there)
                 * gate(rank_across, rank_mine, far))
        w_end = (gate(rank_mine, rank_near, own) * gate(rank_peer, rank_near, there)
                 * gate(rank_across, rank_near, far))
        for c in range(3):
            mine[c, r, :] = w_own * part[c, r, :] + w_end * ends[c, r, :]
        fin[3, r, :] = 1.0 - (own * end) * (there * far)

    def done(s):
        r = at_rows(s)
        for c in range(3):
            fin[c, r, :] = mine[c, r, :] + theirs[c, r, :]

    @pl.when(is_mid)
    def _():
        def stage(it, _):
            @pl.when(it < STRIPS)
            def _():
                compute(it)
                send_part(it).wait_recv()
                send_far(it).wait_recv()
                send_own(it).wait_recv()
                sums(it)
                send_sum(it).start()
                send_opac(it).start()
                opac_out(it).start()

            @pl.when(it >= LAG_DONE)
            def _():
                s = it - LAG_DONE
                send_sum(s).wait_recv()
                done(s)
                send_fin(s).start()
                rgb_out(s).start()
            return 0
        lax.fori_loop(0, STRIPS + LAG_DONE, stage, 0)

        def last(s, _):
            send_own(s).wait_send()
            send_far(s).wait_send()
            send_sum(s).wait_send()
            send_opac(s).wait_send()
            send_fin(s).wait_send()
            opac_out(s).wait()
            rgb_out(s).wait()
            return 0
        lax.fori_loop(0, STRIPS, last, 0)


def on_device(n_depth, n_lat, scalar_field, bin_index, sample_counts, view_order, light_dir,
              tf_color, tf_opacity):
    exchange = n_depth == 4
    planes, rows, cols = bin_index.shape[1:]
    image = (4, rows, cols)
    dma = pltpu.SemaphoreType.DMA
    hbm = pl.BlockSpec(memory_space=pltpu.HBM)
    f32 = jnp.float32
    result = pl.pallas_call(
        functools.partial(kernel, n_depth, n_lat, exchange),
        out_shape=jax.ShapeDtypeStruct(image, f32),
        in_specs=[hbm] * 7,
        out_specs=pl.BlockSpec(memory_space=pl.ANY),
        scratch_shapes=[
            pltpu.SMEM(sample_counts.shape, jnp.int32),
            pltpu.SMEM(view_order.shape, jnp.int32),
            pltpu.SMEM(light_dir.shape, f32),
            pltpu.VMEM(tf_color.shape, f32),
            pltpu.VMEM(tf_opacity.shape, f32),
            dma((5,)),
            pltpu.VMEM((2, planes + 2, rows + 16, LANES), f32),
            pltpu.VMEM((2, planes, rows, LANES), jnp.int32),
            pltpu.VMEM((rows, LANES), f32),
            pltpu.VMEM((rows, LANES), f32),
            pltpu.VMEM((2, 2, planes, LANES), f32),
            pltpu.VMEM((2, 2, planes, LANES), f32),
            pltpu.VMEM((4, 8, LANES), f32),
            pltpu.VMEM(image, f32),
            pltpu.VMEM(image, f32),
            pltpu.VMEM((2, rows, cols), f32),
            pltpu.VMEM((3, rows, cols), f32),
            pltpu.VMEM((3, rows, cols), f32),
            pltpu.VMEM(image, f32),
            dma((CHUNKS, 4)), dma((2,)), dma((4,)),
        ] + [dma((STRIPS,))] * 16,
        compiler_params=pltpu.CompilerParams(
            collective_id=0, has_side_effects=True, vmem_limit_bytes=60 * 1024 * 1024),
    )(scalar_field, bin_index, sample_counts, view_order, light_dir, tf_color, tf_opacity)
    if exchange:
        return result
    return composite(lax.all_gather(result[None], "depth", axis=0, tiled=True), view_order)


def solution(mesh):
    return jax.shard_map(
        functools.partial(on_device, mesh.shape["depth"], mesh.shape["lat"]),
        mesh=mesh,
        in_specs=(
            P(("groups", "depth"), None, "lat", "sub"),
            P(("groups", "depth"), None, "lat", "sub"),
            P(("groups", "depth"), "lat", "sub"),
            P("groups"),
            P(),
            P(),
            P(),
        ),
        out_specs=P(None, ("groups", "lat"), "sub"),
        check_vma=False,
    )
```

```python
import functools
import math

import jax
import jax.numpy as jnp
from jax import lax
from jax.experimental import pallas as pl
from jax.experimental.pallas import tpu as pltpu
from jax.sharding import PartitionSpec as P

MESH = pl.DeviceIdType.MESH
LANES = 128
STRIPS = 16
CHUNKS = 4
LAG_DONE = 4


def composite(stacked, view_order):
    image_rgb = jnp.zeros((3,) + stacked.shape[2:], jnp.float32)
    image_remain = jnp.ones(stacked.shape[2:], jnp.float32)

    def one_brick(rank_idx, state):
        accum_rgb, remain = state
        partial_value = lax.dynamic_index_in_dim(stacked, view_order[rank_idx], 0, keepdims=False)
        return (accum_rgb + remain * partial_value[:3], remain * partial_value[3])

    image_rgb, image_remain = lax.fori_loop(
        0, stacked.shape[0], one_brick, (image_rgb, image_remain)
    )
    return jnp.concatenate([image_rgb, (1.0 - image_remain)[None]], 0)


def lookup(table, bins):
    return jnp.take_along_axis(table, bins, axis=1, mode="promise_in_bounds")


def kernel(
    n_depth, n_lat, exchange,
    field, bins, counts_in, order_in, light_in, color_in, opacity_in, out,
    counts, order, light, color, opacity, small_sem, fv, bv, col_send, col_recv, row_send, row_recv, table,
    part, ends, far_remain, mine, theirs, fin,
    load_sem, col_sem, row_sem,
    part_sems, part_recv, own_sems, own_recv, end_sems, end_recv, far_sems, far_recv,
    sum_sems, sum_recv, opac_sems, opac_recv, fin_sems, fin_recv, out_sems, out_opac_sems,
):
    planes = bv.shape[1]
    rows = bv.shape[2]
    strip = rows // STRIPS
    z = lax.axis_index("depth")
    lat = lax.axis_index("lat")
    sub = lax.axis_index("sub")

    small = [
        pltpu.make_async_copy(src, dst, small_sem.at[i])
        for i, (src, dst) in enumerate((
            (counts_in, counts), (order_in, order), (light_in, light),
            (color_in, color), (opacity_in, opacity)))
    ]
    for load in small:
        load.start()

    chunk_rows = rows // CHUNKS
    loads = []
    for c in range(CHUNKS):
        for t in range(2):
            loads.append(pltpu.make_async_copy(
                field.at[0, :, pl.ds(c * chunk_rows, chunk_rows), pl.ds(t * LANES, LANES)],
                fv.at[t, :, pl.ds(8 + c * chunk_rows, chunk_rows), :], load_sem.at[c, t]))
            loads.append(pltpu.make_async_copy(
                bins.at[0, :, pl.ds(c * chunk_rows, chunk_rows), pl.ds(t * LANES, LANES)],
                bv.at[t, :, pl.ds(c * chunk_rows, chunk_rows), :], load_sem.at[c, 2 + t]))
    for load in loads:
        load.start()

    barrier = pltpu.get_barrier_semaphore()
    pl.semaphore_signal(barrier, inc=1, device_id={"sub": 1 - sub}, device_id_type=MESH)
    has_up = lat > 0
    has_down = lat < n_lat - 1

    @pl.when(has_up)
    def _():
        pl.semaphore_signal(barrier, inc=1, device_id={"lat": lat - 1}, device_id_type=MESH)

    @pl.when(has_down)
    def _():
        pl.semaphore_signal(barrier, inc=1, device_id={"lat": lat + 1}, device_id_type=MESH)

    greet = 1 + has_up.astype(jnp.int32) + has_down.astype(jnp.int32)
    is_end = jnp.logical_or(z == 0, z == 3)
    is_mid = jnp.logical_not(is_end)
    near = jnp.where(z == 0, 1, jnp.where(z == 1, 0, jnp.where(z == 2, 3, 2)))
    peer = 3 - z
    across = 3 - near
    if exchange:
        pl.semaphore_signal(barrier, inc=1, device_id={"depth": near}, device_id_type=MESH)

        @pl.when(is_mid)
        def _():
            pl.semaphore_signal(barrier, inc=1, device_id={"depth": peer}, device_id_type=MESH)

        greet = greet + 1 + is_mid.astype(jnp.int32)

    lane = lax.broadcasted_iota(jnp.int32, (8, LANES), 1)
    wide_lane = lax.broadcasted_iota(jnp.int32, (32, LANES), 1)
    first_lane = lane == 0
    last_lane = lane == LANES - 1

    for load in small:
        load.wait()
    table[...] = jnp.zeros_like(table)
    n_bins = color.shape[1]
    for c in range(3):
        table[c, :, 0:n_bins] = jnp.broadcast_to(color[c:c + 1, :], (8, n_bins))
    table[3, :, 0:n_bins] = jnp.broadcast_to(
        opacity[...].reshape(1, n_bins), (8, n_bins)) * (-1.0 / math.log(2.0))

    count = counts[0, 0, 0]

    def at_rows(s):
        return pl.ds(pl.multiple_of(s * strip, strip), strip)

    def send_own(s):
        return pltpu.make_async_remote_copy(
            src_ref=part.at[3, at_rows(s), :], dst_ref=far_remain.at[0, at_rows(s), :],
            send_sem=own_sems.at[s], recv_sem=own_recv.at[s],
            device_id={"depth": peer}, device_id_type=MESH)

    def send_end(s):
        return pltpu.make_async_remote_copy(
            src_ref=part.at[3, at_rows(s), :], dst_ref=ends.at[3, at_rows(s), :],
            send_sem=end_sems.at[s], recv_sem=end_recv.at[s],
            device_id={"depth": near}, device_id_type=MESH)

    def send_far(s):
        return pltpu.make_async_remote_copy(
            src_ref=ends.at[3, at_rows(s), :], dst_ref=far_remain.at[1, at_rows(s), :],
            send_sem=far_sems.at[s], recv_sem=far_recv.at[s],
            device_id={"depth": peer}, device_id_type=MESH)

    def survive_all(s, _):
        def group(i, _):
            r0 = pl.multiple_of(s * strip + i * 8, 8)
            for t in range(2):
                power = jnp.zeros((8, LANES), jnp.float32)
                for k in range(planes):
                    extinct_k = jnp.where(k < count, table[3], 0.0)
                    soft = jnp.log(1.0 + jnp.exp(fv[t, k + 1, pl.ds(8 + r0, 8), :]))
                    power = power + lookup(extinct_k, bv[t, k, pl.ds(r0, 8), :]) * soft
                part[3, pl.ds(r0, 8), t * LANES:(t + 1) * LANES] = jnp.exp2(power)
            return 0
        lax.fori_loop(0, strip // 8, group, 0)
        if exchange:
            @pl.when(is_end)
            def _():
                send_end(s).start()

            @pl.when(is_mid)
            def _():
                send_own(s).start()
        return 0

    def remains(c):
        for load in loads[4 * c:4 * c + 4]:
            load.wait()
        lax.fori_loop(c * STRIPS // CHUNKS, (c + 1) * STRIPS // CHUNKS, survive_all, 0)

    pl.semaphore_wait(barrier, greet)
    for c in range(CHUNKS // 2):
        remains(c)
    for load in loads[2 * CHUNKS:]:
        load.wait()

    for t in range(2):
        for k in range(planes):
            row_send[0, t, k:k + 1, :] = fv[t, k + 1, 8:9, :]
            row_send[1, t, k:k + 1, :] = fv[t, k + 1, 7 + rows:8 + rows, :]

    up = pltpu.make_async_remote_copy(
        src_ref=row_send.at[0], dst_ref=row_recv.at[1], send_sem=row_sem.at[0],
        recv_sem=row_sem.at[2], device_id={"lat": lat - 1}, device_id_type=MESH)
    down = pltpu.make_async_remote_copy(
        src_ref=row_send.at[1], dst_ref=row_recv.at[0], send_sem=row_sem.at[1],
        recv_sem=row_sem.at[3], device_id={"lat": lat + 1}, device_id_type=MESH)

    @pl.when(has_up)
    def _():
        up.start()

    @pl.when(has_down)
    def _():
        down.start()

    def pack(src, offset):
        def chunk(i, _):
            r0 = pl.multiple_of(i * 32, 32)
            packed = jnp.zeros((32, LANES), jnp.float32)
            for k in range(planes):
                to = (2 * k + offset) % LANES
                shift = (to + 1) % LANES if src == 1 else to
                value = fv[src, k + 1, pl.ds(8 + r0, 32), :]
                if shift:
                    value = pltpu.roll(value, shift, 1)
                packed = jnp.where(wide_lane == to, value, packed)
            col_send[pl.ds(r0, 32), :] = packed
            return 0
        lax.fori_loop(0, rows // 32, chunk, 0)

    @pl.when(sub == 0)
    def _():
        pack(1, 0)

    @pl.when(sub == 1)
    def _():
        pack(0, -1)

    side = pltpu.make_async_remote_copy(
        src_ref=col_send, dst_ref=col_recv, send_sem=col_sem.at[0],
        recv_sem=col_sem.at[1], device_id={"sub": 1 - sub}, device_id_type=MESH)
    side.start()

    for c in range(CHUNKS // 2, CHUNKS):
        lax.fori_loop(c * STRIPS // CHUNKS, (c + 1) * STRIPS // CHUNKS, survive_all, 0)

    @pl.when(has_up)
    def _():
        up.wait_send()
        down.wait_recv()

    @pl.when(has_down)
    def _():
        down.wait_send()
        up.wait_recv()

    @pl.when(jnp.logical_not(has_up))
    def _():
        row_recv[0] = jnp.zeros(row_recv.shape[1:], jnp.float32)

    @pl.when(jnp.logical_not(has_down))
    def _():
        row_recv[1] = jnp.zeros(row_recv.shape[1:], jnp.float32)

    for t in range(2):
        for k in range(planes):
            fv[t, k + 1, 7:8, :] = row_recv[0, t, k:k + 1, :]
            fv[t, k + 1, 8 + rows:9 + rows, :] = row_recv[1, t, k:k + 1, :]

    side.wait()

    lx = light[0] * 0.5
    ly = light[1] * 0.5
    lz = light[2] * 0.5

    def march(r0):
        halo = col_recv[pl.ds(r0, 8), :]
        before = [fv[t, 0, pl.ds(8 + r0, 8), :] for t in range(2)]
        here = [fv[t, 1, pl.ds(8 + r0, 8), :] for t in range(2)]
        total = [[jnp.zeros((8, LANES), jnp.float32) for _ in range(3)] for _ in range(2)]
        remain = [jnp.ones((8, LANES), jnp.float32) for _ in range(2)]
        colors = [table[c] for c in range(3)]
        extinct = table[3]
        for k in range(planes):
            after = [fv[t, k + 2, pl.ds(8 + r0, 8), :] for t in range(2)]
            extinct_k = jnp.where(k < count, extinct, 0.0)
            up1 = [pltpu.roll(here[t], 1, 1) for t in range(2)]
            dn1 = [pltpu.roll(here[t], LANES - 1, 1) for t in range(2)]
            edge = pltpu.roll(halo, (LANES - 2 * k) % LANES, 1) if k else halo
            minus = [jnp.where(first_lane, edge, up1[0]), jnp.where(first_lane, up1[0], up1[1])]
            plus = [jnp.where(last_lane, dn1[1], dn1[0]), jnp.where(last_lane, edge, dn1[1])]
            for t in range(2):
                gx = fv[t, k + 1, pl.ds(9 + r0, 8), :] - fv[t, k + 1, pl.ds(7 + r0, 8), :]
                gy = plus[t] - minus[t]
                gz = after[t] - before[t]
                dot = gx * lx + gy * ly + gz * lz
                norm = gx * gx + gy * gy + (gz * gz + 4.0)
                shading = jnp.abs(dot * lax.rsqrt(norm)) + 0.25
                soft = jnp.log(1.0 + jnp.exp(here[t]))
                bin_ids = bv[t, k, pl.ds(r0, 8), :]
                survive = jnp.exp2(lookup(extinct_k, bin_ids) * soft)
                left_over = remain[t] * survive
                weight = (remain[t] - left_over) * shading
                for c in range(3):
                    total[t][c] = total[t][c] + weight * lookup(colors[c], bin_ids)
                remain[t] = left_over
            before, here = here, after
        for t in range(2):
            for c in range(3):
                part[c, pl.ds(r0, 8), t * LANES:(t + 1) * LANES] = total[t][c]

    def compute(s):
        def group(i, _):
            march(pl.multiple_of(s * strip + i * 8, 8))
            return 0
        lax.fori_loop(0, strip // 8, group, 0)

    def to_out(s, src):
        return pltpu.make_async_copy(
            src.at[:, at_rows(s), :], out.at[:, at_rows(s), :], out_sems.at[s])

    if not exchange:
        def plain(s, _):
            compute(s)
            to_out(s, part).start()
            return 0
        lax.fori_loop(0, STRIPS, plain, 0)

        def finish(s, _):
            to_out(s, part).wait()
            return 0
        lax.fori_loop(0, STRIPS, finish, 0)
        return

    def send_part(s):
        return pltpu.make_async_remote_copy(
            src_ref=part.at[0:3, at_rows(s), :], dst_ref=ends.at[0:3, at_rows(s), :],
            send_sem=part_sems.at[s], recv_sem=part_recv.at[s],
            device_id={"depth": near}, device_id_type=MESH)

    def send_sum(s):
        return pltpu.make_async_remote_copy(
            src_ref=mine.at[:, at_rows(s), :], dst_ref=theirs.at[:, at_rows(s), :],
            send_sem=sum_sems.at[s], recv_sem=sum_recv.at[s],
            device_id={"depth": peer}, device_id_type=MESH)

    def send_fin(s):
        return pltpu.make_async_remote_copy(
            src_ref=fin.at[0:3, at_rows(s), :], dst_ref=out.at[0:3, at_rows(s), :],
            send_sem=fin_sems.at[s], recv_sem=fin_recv.at[s],
            device_id={"depth": near}, device_id_type=MESH)

    def send_opac(s):
        return pltpu.make_async_remote_copy(
            src_ref=fin.at[3, at_rows(s), :], dst_ref=out.at[3, at_rows(s), :],
            send_sem=opac_sems.at[s], recv_sem=opac_recv.at[s],
            device_id={"depth": near}, device_id_type=MESH)

    def rgb_out(s):
        return pltpu.make_async_copy(
            fin.at[0:3, at_rows(s), :], out.at[0:3, at_rows(s), :], out_sems.at[s])

    def opac_out(s):
        return pltpu.make_async_copy(
            fin.at[3, at_rows(s), :], out.at[3, at_rows(s), :], out_opac_sems.at[s])

    @pl.when(is_end)
    def _():
        def first(s, _):
            compute(s)
            send_part(s).start()
            return 0
        lax.fori_loop(0, STRIPS, first, 0)

        def last(s, _):
            send_end(s).wait_send()
            send_part(s).wait_send()
            send_opac(s).wait_recv()
            send_fin(s).wait_recv()
            return 0
        lax.fori_loop(0, STRIPS, last, 0)

    def rank_of(brick):
        rank = jnp.int32(0)
        for r in range(1, n_depth):
            rank = rank + jnp.where(order[r] == brick, r, 0)
        return rank

    rank_mine = rank_of(z)
    rank_near = rank_of(near)
    rank_peer = rank_of(peer)
    rank_across = rank_of(across)

    def gate(a, b, value):
        return jnp.where(a < b, value, jnp.ones_like(value))

    def sums(s):
        r = at_rows(s)
        own = part[3, r, :]
        end = ends[3, r, :]
        there = far_remain[0, r, :]
        far = far_remain[1, r, :]
        w_own = (gate(rank_near, rank_mine, end) * gate(rank_peer, rank_mine, there)
                 * gate(rank_across, rank_mine, far))
        w_end = (gate(rank_mine, rank_near, own) * gate(rank_peer, rank_near, there)
                 * gate(rank_across, rank_near, far))
        for c in range(3):
            mine[c, r, :] = w_own * part[c, r, :] + w_end * ends[c, r, :]
        fin[3, r, :] = (own * end) * (there * far)

    def done(s):
        r = at_rows(s)
        for c in range(3):
            fin[c, r, :] = mine[c, r, :] + theirs[c, r, :]

    @pl.when(is_mid)
    def _():
        def stage(it, _):
            @pl.when(it < STRIPS // 2)
            def _():
                for s in range(2):
                    send_end(2 * it + s).wait_recv()
                    send_far(2 * it + s).start()

            @pl.when(it < STRIPS)
            def _():
                compute(it)
                send_part(it).wait_recv()
                send_far(it).wait_recv()
                send_own(it).wait_recv()
                sums(it)
                send_sum(it).start()
                send_opac(it).start()
                opac_out(it).start()

            @pl.when(it >= LAG_DONE)
            def _():
                s = it - LAG_DONE
                send_sum(s).wait_recv()
                done(s)
                send_fin(s).start()
                rgb_out(s).start()
            return 0
        lax.fori_loop(0, STRIPS + LAG_DONE, stage, 0)

        def last(s, _):
            send_own(s).wait_send()
            send_far(s).wait_send()
            send_sum(s).wait_send()
            send_opac(s).wait_send()
            send_fin(s).wait_send()
            opac_out(s).wait()
            rgb_out(s).wait()
            return 0
        lax.fori_loop(0, STRIPS, last, 0)


def on_device(n_depth, n_lat, scalar_field, bin_index, sample_counts, view_order, light_dir,
              tf_color, tf_opacity):
    exchange = n_depth == 4
    planes, rows, cols = bin_index.shape[1:]
    image = (4, rows, cols)
    dma = pltpu.SemaphoreType.DMA
    hbm = pl.BlockSpec(memory_space=pltpu.HBM)
    f32 = jnp.float32
    result = pl.pallas_call(
        functools.partial(kernel, n_depth, n_lat, exchange),
        out_shape=jax.ShapeDtypeStruct(image, f32),
        in_specs=[hbm] * 7,
        out_specs=pl.BlockSpec(memory_space=pl.ANY),
        scratch_shapes=[
            pltpu.SMEM(sample_counts.shape, jnp.int32),
            pltpu.SMEM(view_order.shape, jnp.int32),
            pltpu.SMEM(light_dir.shape, f32),
            pltpu.VMEM(tf_color.shape, f32),
            pltpu.VMEM(tf_opacity.shape, f32),
            dma((5,)),
            pltpu.VMEM((2, planes + 2, rows + 16, LANES), f32),
            pltpu.VMEM((2, planes, rows, LANES), jnp.int32),
            pltpu.VMEM((rows, LANES), f32),
            pltpu.VMEM((rows, LANES), f32),
            pltpu.VMEM((2, 2, planes, LANES), f32),
            pltpu.VMEM((2, 2, planes, LANES), f32),
            pltpu.VMEM((4, 8, LANES), f32),
            pltpu.VMEM(image, f32),
            pltpu.VMEM(image, f32),
            pltpu.VMEM((2, rows, cols), f32),
            pltpu.VMEM((3, rows, cols), f32),
            pltpu.VMEM((3, rows, cols), f32),
            pltpu.VMEM(image, f32),
            dma((CHUNKS, 4)), dma((2,)), dma((4,)),
        ] + [dma((STRIPS,))] * 16,
        compiler_params=pltpu.CompilerParams(
            collective_id=0, has_side_effects=True, vmem_limit_bytes=60 * 1024 * 1024),
    )(scalar_field, bin_index, sample_counts, view_order, light_dir, tf_color, tf_opacity)
    if exchange:
        channel = lax.broadcasted_iota(jnp.int32, result.shape, 0)
        return jnp.where(channel == 3, 1.0 - result, result)
    return composite(lax.all_gather(result[None], "depth", axis=0, tiled=True), view_order)


def solution(mesh):
    return jax.shard_map(
        functools.partial(on_device, mesh.shape["depth"], mesh.shape["lat"]),
        mesh=mesh,
        in_specs=(
            P(("groups", "depth"), None, "lat", "sub"),
            P(("groups", "depth"), None, "lat", "sub"),
            P(("groups", "depth"), "lat", "sub"),
            P("groups"),
            P(),
            P(),
            P(),
        ),
        out_specs=P(None, ("groups", "lat"), "sub"),
        check_vma=False,
    )
```
